32 devices in a mesh: space: 16 (over z, y, core), dom: 2 (over x).
Axes of the slice: x: 2, y: 2, z: 4, core: 2. Of those that a mesh axis runs over, the one named last changes fastest.
Arguments:
- water_depth: float32 [4, 16, 256, 512], P('dom', 'space'), may hold values from 0 to 1.5
- infiltrated: float32 [4, 16, 256, 512], P('dom', 'space'), may hold values from 0.2 to 2
- terrain: float32 [16, 256, 512], P('space'), may hold values from -3 to 3
- land_mask: int32 [16, 256, 512], P('space'), may hold values from 0 to 1
- forcing: bfloat16 [2, 2, 16, 256, 512], P(None, None, 'space', 'dom'), may hold values from 0.049804688 to 1.5
- observed: bfloat16 [2, 16, 256, 512], P(None, 'space'), may hold values from 0 to 3.6
- conductivity: float32 [4], replicated, may hold values from 0.05 to 0.6
- suction: float32 [4], replicated, may hold values from 0.1 to 2
- manning: float32 [4], replicated, may hold values from 0.5 to 2
- assignment: int32 [4], P('dom'), may hold values from 0 to 3, each once
- ancestors: int32 [4], P('dom'), may hold values from 0 to 3, as said below
- prior_weight: float32 [4], P('dom'), may hold values from 0.01 to 1
Outputs:
- final_depth: float32 [4, 16, 256, 512], P('dom', 'space')
- final_infiltrated: float32 [4, 16, 256, 512], P('dom', 'space')
- weights: float32 [4], P('dom')
The draws below stay inside these ranges and needn't reach their ends.
Inputs may be any that keep to these rules, and one draw needn't show every extreme that they name: `ancestors`: the ancestor of slot s is a slot of its own group, 2 * (s // 2) to 2 * (s // 2) + 1; slot 0's ancestor is 0 and the last slot's is itself.
All inputs are finite; a program needn't handle non-finite values.
Results may differ from the reference program's by a relative error of at most 0.0003.
Values may be sent and summed in bfloat16 or wider, within the bound.
A program may use at most 64 MiB of HBM per device.

```python
import math
import jax
import jax.numpy as jnp
from jax import lax

CY = 256
CX = 512
P_DEV = 2
TX = 4
SUB = 6
HOURS = 2
PARTS_SIZE = 4
TILES = 16
TY = 4
N_DOM = 2


def draw_land_mask(key, part):
    tiles = jnp.arange(TILES, dtype=jnp.int32)[:, None, None]
    limit = 300 + 600 * tiles // max(TILES - 1, 1)
    roll = jax.random.randint(key, (TILES, CY, CX), 0, 1000)
    return (roll < limit).astype(jnp.int32)


def draw_observed(key, part):
    shape = (HOURS, TILES, CY, CX)
    tiles = jnp.arange(TILES, dtype=jnp.float32)[None, :, None, None]
    scale = 1.0 + 2.0 * tiles / max(TILES - 1, 1)
    base = jax.random.uniform(key, shape, jnp.float32, 0.0, 1.2)
    return (base * scale).astype(jnp.bfloat16)


def draw_ancestors(key, part):
    offsets = jax.random.randint(key, (PARTS_SIZE,), 0, P_DEV)
    offsets = offsets.at[0].set(0).at[PARTS_SIZE - 1].set(P_DEV - 1)
    slots = jnp.arange(PARTS_SIZE, dtype=jnp.int32)
    return slots // P_DEV * P_DEV + offsets


def levels(key, shape, split, low, high):
    level, own = 1.0, jax.random.fold_in(key, 6)
    for axis_at, blocks in split:
        steps = jnp.exp(jax.random.uniform(jax.random.fold_in(own, axis_at), (blocks,), jnp.float32, low / len(split), high / len(split)))
        level = level * jnp.repeat(steps, shape[axis_at] // blocks).reshape([-1 if axis == axis_at else 1 for axis in range(len(shape))])
    return level


def centred(rng, extent, deviation, bound, pieces=(), kind=jnp.bfloat16):
    drawn = deviation * jax.random.normal(rng, extent, jnp.float32)
    if pieces:
        drawn = drawn * levels(rng, extent, pieces, -0.22, 0.18)
    return jnp.clip(drawn, -bound, bound).astype(kind)


def setup_inputs(seed: int = 0) -> dict:
    key_list = jax.random.split(jax.random.key(seed), 13)
    return {
        "water_depth": jnp.clip(1.5 * jax.random.uniform(key_list[0], (PARTS_SIZE, TILES, CY, CX), jnp.float32) ** levels(key_list[0], (PARTS_SIZE, TILES, CY, CX), ((0, 2), (1, 16)), -0.2, 0.2), 0.0, 1.5),
        "infiltrated": jnp.clip(0.2 + 1.8 * jax.random.uniform(key_list[1], (PARTS_SIZE, TILES, CY, CX), jnp.float32) ** levels(key_list[1], (PARTS_SIZE, TILES, CY, CX), ((0, 2), (1, 16)), -0.2, 0.2), 0.2, 2.0),
        "terrain": centred(key_list[2], (TILES, CY, CX), 0.5, 3.0, ((0, 16),), jnp.float32),
        "land_mask": draw_land_mask(jax.random.fold_in(key_list[12], 71), 0),
        "forcing": jnp.clip(jnp.exp(math.log(1.5) - 3.4051113 * jax.random.uniform(key_list[4], (HOURS, 2, TILES, CY, CX), jnp.float32) ** levels(key_list[4], (HOURS, 2, TILES, CY, CX), ((2, 16), (3, 2)), -0.2, 0.2)), 0.049804688, 1.5).astype(jnp.bfloat16),
        "observed": draw_observed(jax.random.fold_in(key_list[12], 71), 0),
        "conductivity": jnp.clip(jnp.exp(jax.random.uniform(key_list[6], (PARTS_SIZE,), jnp.float32, math.log(0.05), math.log(0.6))), 0.05, 0.6),
        "suction": jnp.clip(jnp.exp(jax.random.uniform(key_list[7], (PARTS_SIZE,), jnp.float32, math.log(0.1), math.log(2.0))), 0.1, 2.0),
        "manning": jnp.clip(jnp.exp(jax.random.uniform(key_list[8], (PARTS_SIZE,), jnp.float32, math.log(0.5), math.log(2.0))), 0.5, 2.0),
        "assignment": jax.random.permutation(key_list[9], PARTS_SIZE).astype(jnp.int32),
        "ancestors": draw_ancestors(jax.random.fold_in(key_list[12], 71), 0),
        "prior_weight": jnp.clip(jnp.exp(math.log(1.0) - 4.6051702 * jax.random.uniform(key_list[11], (PARTS_SIZE,), jnp.float32) ** levels(key_list[11], (PARTS_SIZE,), ((0, 2),), -0.2, 0.2)), 0.01, 1.0),
    }


time_step = 0.01
slope_floor = 0.1
sharpness = 20.0

def to_grid(tiles):
    lead = tiles.shape[:-3]
    count = len(lead)
    blocks = tiles.reshape(lead + (TY, TX, CY, CX))
    blocks = jnp.swapaxes(blocks, count + 1, count + 2)
    return blocks.reshape(lead + (TY * CY, TX * CX))

def to_tiles(grid):
    lead = grid.shape[:-2]
    count = len(lead)
    blocks = grid.reshape(lead + (TY, CY, TX, CX))
    blocks = jnp.swapaxes(blocks, count + 1, count + 2)
    return blocks.reshape(lead + (TY * TX, CY, CX))

def pad_field(field):
    tall = jnp.pad(field, ((1, 1), (0, 0)))
    return jnp.pad(tall, ((0, 0), (1, 1)), mode='wrap')

def face_flux(depth_a, depth_b, level_a, level_b, rough):
    slope = level_b - level_a
    mean_depth = 0.5 * (depth_a + depth_b)
    return -jnp.power(mean_depth, 5.0 / 3.0) * slope / (rough * jnp.sqrt(jnp.abs(slope) + slope_floor))

def substep(water, soaked, ground, net_rain, land, conduct, suction_p, rough):
    padded = pad_field(water)
    level = padded + ground
    flux_cols = face_flux(padded[1:-1, :-1], padded[1:-1, 1:], level[1:-1, :-1], level[1:-1, 1:], rough)
    flux_rows = face_flux(padded[:-1, 1:-1], padded[1:, 1:-1], level[:-1, 1:-1], level[1:, 1:-1], rough)
    outflow = flux_cols[:, 1:] - flux_cols[:, :-1] + flux_rows[1:, :] - flux_rows[:-1, :]
    ponded = jnp.maximum(water - time_step * outflow + time_step * net_rain, 0.0)
    capacity = conduct * (1.0 + suction_p / soaked)
    intake = jnp.minimum(time_step * capacity, ponded)
    return ((ponded - intake) * land, soaked + intake * land)

def reference(water_depth, infiltrated, terrain, land_mask, forcing, observed, conductivity, suction, manning, assignment, ancestors, prior_weight):
    owners = assignment[ancestors]
    group_mean = jnp.repeat(lax.optimization_barrier(jnp.mean(prior_weight.reshape(N_DOM, P_DEV), axis=1)), P_DEV)
    land = to_grid(land_mask).astype(jnp.float32)
    ground = pad_field(to_grid(terrain))
    rains = [to_grid(forcing[hour, 0].astype(jnp.float32) - forcing[hour, 1].astype(jnp.float32)) for hour in range(HOURS)]
    seen = [to_grid(observed[hour].astype(jnp.float32)) for hour in range(HOURS)]

    def particle(items):
        water_tiles, soak_tiles, conduct, suction_p, rough = items
        water = to_grid(water_tiles)
        soaked = to_grid(soak_tiles)
        misfit = jnp.zeros((), jnp.float32)
        for hour in range(HOURS):
            net_rain = rains[hour]

            def advance(index, carry):
                return substep(carry[0], carry[1], ground, net_rain, land, conduct, suction_p, rough)
            water, soaked = lax.fori_loop(0, SUB, advance, (water, soaked))
            gap = water - seen[hour]
            square = gap * gap
            misfit = misfit + jnp.sum(land * square / (1.0 + square))
        return (to_tiles(water), to_tiles(soaked), misfit)
    final_depth, final_soak, misfit = lax.map(particle, (water_depth[ancestors], infiltrated[ancestors], conductivity[owners], suction[owners], manning[owners]))
    cells = HOURS * jnp.sum(land)
    raw = group_mean * jnp.exp(-sharpness * misfit / cells)
    weights = raw / jnp.sum(raw)
    return (final_depth, final_soak, weights)
```

```python
import functools
import math

import jax
import jax.numpy as jnp
from jax import lax
from jax.experimental import pallas as pl
from jax.experimental.pallas import tpu as pltpu
from jax.sharding import PartitionSpec as P

TX = 4
SUB = 6
MESH = pl.DeviceIdType.MESH

time_step = 0.01
slope_floor = 0.1
sharpness = 20.0
DRY = -1e30
LANES = 128
ROWS = 8


def passed_along(block, axis, distance):
    devices = range(lax.axis_size(axis))
    route = [(i - distance, i) for i in devices if i - distance in devices]
    return lax.ppermute(block, axis, route)


def passed_along_2(array, axis, by):
    devices = lax.axis_size(axis)
    return lax.ppermute(array, axis, [(i, (i + by) % devices) for i in range(devices)])


def from_west(edge, column_tile):
    near = passed_along_2(edge, "space", 1)
    far = passed_along_2(edge, "space", -(TX - 1))
    return jnp.where(column_tile == 0, far, near)


def from_east(edge, column_tile):
    near = passed_along_2(edge, "space", -1)
    far = passed_along_2(edge, "space", TX - 1)
    return jnp.where(column_tile == TX - 1, far, near)


def face(depth_sum, slope):
    power = jnp.exp2(jnp.log(depth_sum) * (5.0 / 3.0 / math.log(2.0)))
    return power * slope * lax.rsqrt(jnp.abs(slope) + slope_floor)


def window_kernel(
    hours, width, rim, par_ref, d_in, s_in, g_ref, r_ref, obs_ref,
    depth_out, soak_out, miss_out, d_ref, s_ref, ge_ref, gs_ref,
):
    parts, high, wide = d_in.shape
    own_rows, own_cols = depth_out.shape[1:]
    cols = wide // LANES
    blocks = high // ROWS
    top = rim // ROWS
    bottom = top + own_rows // ROWS
    lane = lax.broadcasted_iota(jnp.int32, (ROWS, LANES), 1)
    sub = lax.broadcasted_iota(jnp.int32, (ROWS, LANES), 0)
    first_lane, last_lane = lane == 0, lane == LANES - 1
    first_sub, last_sub = sub == 0, sub == ROWS - 1

    def at(block, j):
        return pl.ds(pl.multiple_of(block * ROWS, ROWS), ROWS), pl.ds(j * LANES, LANES)

    def east(here, beside):
        return pltpu.roll(jnp.where(first_lane, beside, here), LANES - 1, 1)

    def south(here, below):
        return pltpu.roll(jnp.where(first_sub, below, here), ROWS - 1, 0)

    def prepare(block, carry):
        below = jnp.minimum(block + 1, blocks - 1)
        for j in range(cols):
            here = g_ref[at(block, j)]
            ge_ref[at(block, j)] = east(here, g_ref[at(block, (j + 1) % cols)]) - here
            gs_ref[at(block, j)] = south(here, g_ref[at(below, j)]) - here
            for p in range(parts):
                d_ref[(p,) + at(block, j)] = d_in[(p,) + at(block, j)]
                s_ref[(p,) + at(block, j)] = s_in[(p,) + at(block, j)]
        return carry

    lax.fori_loop(0, blocks, prepare, 0)
    for p in range(parts):
        d_ref[p, pl.ds(high, ROWS), :] = jnp.zeros((ROWS, wide), jnp.float32)

    for hour in range(hours):

        def substep(index, carry):
            left = hours * SUB - 1 - (hour * SUB + index)
            start = top - 1 - left // ROWS
            stop = bottom + (left + ROWS - 1) // ROWS

            def step(block, above):
                out = []
                for p in range(parts):
                    k, a, b = par_ref[0, p], par_ref[1, p], par_ref[2, p]
                    d = [d_ref[(p,) + at(block, j)] for j in range(cols)]

                    def col_face(j):
                        d_e = east(d[j], d[(j + 1) % cols])
                        return face(d[j] + d_e, (d_e - d[j]) + ge_ref[at(block, j)])

                    last = col_face(cols - 1)
                    west = last
                    for j in range(cols):
                        f_e = last if j == cols - 1 else col_face(j)
                        f_w = pltpu.roll(jnp.where(last_lane, west, f_e), 1, 1)
                        west = f_e
                        d_s = south(d[j], d_ref[(p,) + at(block + 1, j)])
                        f_s = face(d[j] + d_s, (d_s - d[j]) + gs_ref[at(block, j)])
                        f_n = pltpu.roll(jnp.where(last_sub, above[p * cols + j], f_s), 1, 0)
                        out.append(f_s)
                        gain = (f_e - f_w) + (f_s - f_n)
                        ponded = jnp.maximum(d[j] + k * gain + r_ref[(hour,) + at(block, j)], 0.0)
                        soak = s_ref[(p,) + at(block, j)]
                        inverse = pl.reciprocal(soak, approx=True)
                        inverse = inverse * (2.0 - soak * inverse)
                        intake = jnp.minimum(a + b * inverse, ponded)
                        d_ref[(p,) + at(block, j)] = ponded - intake
                        s_ref[(p,) + at(block, j)] = soak + intake
                return tuple(out)

            zero = jnp.zeros((ROWS, LANES), jnp.float32)
            lax.fori_loop(start, stop, step, (zero,) * (parts * cols))
            return carry

        lax.fori_loop(0, SUB, substep, 0)

        def score(block, sums):
            sums = list(sums)
            for j in range(own_cols // LANES):
                seen = obs_ref[(hour,) + at(block, j)]
                for p in range(parts):
                    gap = d_ref[(p,) + at(block + top, j)] - seen
                    square = gap * gap
                    sums[p] += jnp.where(seen >= 0.0, square / (1.0 + square), 0.0)
            return tuple(sums)

        zero = jnp.zeros((ROWS, LANES), jnp.float32)
        sums = lax.fori_loop(0, own_rows // ROWS, score, (zero,) * parts)
        for p in range(parts):
            miss_out[p] = sums[p] if hour == 0 else miss_out[p] + sums[p]

    def finish(block, carry):
        for j in range(own_cols // LANES):
            for p in range(parts):
                depth_out[(p,) + at(block, j)] = d_ref[(p,) + at(block + top, j)]
                soak_out[(p,) + at(block, j)] = s_ref[(p,) + at(block + top, j)]
        return carry

    lax.fori_loop(0, own_rows // ROWS, finish, 0)


def weigh_kernel(n_space, n_dom, parts, mine_ref, out_ref, held, send_sem, recv_sem):
    total = n_space * n_dom
    space, dom = lax.axis_index("space"), lax.axis_index("dom")
    me = space * n_dom + dom
    barrier = pltpu.get_barrier_semaphore()

    def place(i):
        other = lax.rem(me + i, total)
        return (other // n_dom, lax.rem(other, n_dom))

    def greet(i, carry):
        pl.semaphore_signal(barrier, inc=1, device_id=place(i), device_id_type=MESH)
        return carry

    lax.fori_loop(1, total, greet, 0)
    pl.semaphore_wait(barrier, total - 1)

    def copy(i):
        return pltpu.make_async_remote_copy(
            src_ref=mine_ref, dst_ref=held.at[i], send_sem=send_sem.at[i], recv_sem=recv_sem.at[i],
            device_id=place(i), device_id_type=MESH,
        )

    def send(i, carry):
        copy(i).start()
        return carry

    def arrive(i, carry):
        copy(i).wait()
        return carry

    lax.fori_loop(1, total, send, 0)
    held[0] = mine_ref[...]
    lax.fori_loop(1, total, arrive, 0)

    def add(i, sums):
        theirs = lax.rem(lax.rem(me - i + total, total), n_dom)
        block = held[i]
        return tuple(s + jnp.where(theirs == g, block, 0.0) for g, s in enumerate(sums))

    zero = jnp.zeros(mine_ref.shape, jnp.float32)
    sums = lax.fori_loop(0, total, add, (zero,) * n_dom)
    whole = jnp.zeros((1, 1), jnp.float32)
    own = zero[0:1]
    lane = lax.broadcasted_iota(jnp.int32, (1, LANES), 1)
    for g in range(n_dom):
        misfit, cells, mean = sums[g][0:1], sums[g][1:2], sums[g][2:3] / n_space
        raw = jnp.where(lane < parts, mean * jnp.exp(-sharpness * misfit / cells), 0.0)
        whole = whole + jnp.sum(raw, axis=1, keepdims=True)
        own = jnp.where(dom == g, raw, own)
    out_ref[...] = jnp.broadcast_to(own / whole, out_ref.shape)


def local(
    n_space, n_dom,
    water_depth, infiltrated, terrain, land_mask, forcing, observed,
    conductivity, suction, manning, assignment, ancestors, prior_weight,
):
    parts, _, rows, columns = water_depth.shape
    hours = observed.shape[0]
    width = hours * SUB
    rim = -(-width // ROWS) * ROWS
    first_slot = lax.axis_index("dom") * parts
    local_slot = ancestors - first_slot
    water = jnp.take(water_depth[:, 0], local_slot, axis=0)
    soaked = jnp.take(infiltrated[:, 0], local_slot, axis=0)
    owners = jnp.take(assignment, local_slot)
    every_slot = jnp.arange(conductivity.shape[0], dtype=jnp.int32)
    picker = owners[:, None] == every_slot[None, :]

    def lookup(table):
        return jnp.sum(jnp.where(picker, table[None, :], 0.0), axis=1)

    conduct, suction_p, rough = lookup(conductivity), lookup(suction), lookup(manning)
    params = jnp.stack(
        [time_step * 0.5 ** (5.0 / 3.0) / rough, time_step * conduct, time_step * conduct * suction_p]
    )
    group_mean = jnp.mean(prior_weight)
    column_tile = lax.axis_index("space") % TX
    row_tile = lax.axis_index("space") // TX
    land = land_mask[0] > 0
    forced = lax.all_gather(forcing, "dom", axis=3, tiled=True)[:, :, 0].astype(jnp.float32)
    rain = jnp.where(land[None], time_step * (forced[:, 0] - forced[:, 1]), DRY)
    fields = jnp.concatenate([water, soaked, terrain, rain], axis=0)
    fill = jnp.array([0.0] * parts + [1.0] * parts + [0.0] + [DRY] * hours, jnp.float32)[:, None, None]
    west = from_west(fields[:, :, -width:], column_tile)
    east = from_east(fields[:, :, :width], column_tile)
    gap = jnp.broadcast_to(fill, (fields.shape[0], rows, LANES - 2 * width))
    wide = jnp.concatenate([fields, east, gap, west], axis=-1)
    north = passed_along(wide[:, -rim:, :], "space", TX)
    south = passed_along(wide[:, :rim, :], "space", -TX)
    north = jnp.where(row_tile == 0, fill, north)
    south = jnp.where(row_tile == n_space // TX - 1, fill, south)
    big = jnp.concatenate([north, wide, south], axis=-2)
    high, across = big.shape[1:]
    seen = jnp.where(land[None], observed[:, 0].astype(jnp.float32), -1.0)
    vmem = pl.BlockSpec(memory_space=pltpu.VMEM)
    depth, soak, missed = pl.pallas_call(
        functools.partial(window_kernel, hours, width, rim),
        out_shape=(
            jax.ShapeDtypeStruct((parts, rows, columns), jnp.float32),
            jax.ShapeDtypeStruct((parts, rows, columns), jnp.float32),
            jax.ShapeDtypeStruct((parts, ROWS, LANES), jnp.float32),
        ),
        in_specs=[pl.BlockSpec(memory_space=pltpu.SMEM)] + [vmem] * 5,
        out_specs=(vmem, vmem, vmem),
        scratch_shapes=[
            pltpu.VMEM((parts, high + ROWS, across), jnp.float32),
            pltpu.VMEM((parts, high, across), jnp.float32),
            pltpu.VMEM((high, across), jnp.float32),
            pltpu.VMEM((high, across), jnp.float32),
        ],
        compiler_params=pltpu.CompilerParams(vmem_limit_bytes=48 * 2**20),
    )(params, big[:parts], big[parts : 2 * parts], big[2 * parts], big[2 * parts + 1 :], seen)
    misfit = jnp.sum(missed, axis=(1, 2))
    cells = hours * jnp.sum(land.astype(jnp.float32))
    mine = jnp.zeros((ROWS, LANES), jnp.float32).at[0, :parts].set(misfit).at[1].set(cells).at[2].set(group_mean)
    total = n_space * n_dom
    weights = pl.pallas_call(
        functools.partial(weigh_kernel, n_space, n_dom, parts),
        out_shape=jax.ShapeDtypeStruct((ROWS, LANES), jnp.float32),
        in_specs=[vmem],
        out_specs=vmem,
        scratch_shapes=[
            pltpu.VMEM((total, ROWS, LANES), jnp.float32),
            pltpu.SemaphoreType.DMA((total,)),
            pltpu.SemaphoreType.DMA((total,)),
        ],
        compiler_params=pltpu.CompilerParams(collective_id=0, has_side_effects=True),
    )(mine)
    return depth[:, None], soak[:, None], weights[0, :parts]


def solution(mesh):
    return jax.shard_map(
        functools.partial(local, mesh.shape["space"], mesh.shape["dom"]),
        mesh=mesh,
        in_specs=(
            P("dom", "space", None, None),
            P("dom", "space", None, None),
            P("space", None, None),
            P("space", None, None),
            P(None, None, "space", "dom", None),
            P(None, "space", None, None),
            P(),
            P(),
            P(),
            P("dom"),
            P("dom"),
            P("dom"),
        ),
        out_specs=(P("dom", "space", None, None), P("dom", "space", None, None), P("dom")),
        check_vma=False,
    )
```

```python
import functools
import math

import jax
import jax.numpy as jnp
from jax import lax
from jax.experimental import pallas as pl
from jax.experimental.pallas import tpu as pltpu
from jax.sharding import PartitionSpec as P

TX = 4
SUB = 6
MESH = pl.DeviceIdType.MESH

time_step = 0.01
slope_floor = 0.1
sharpness = 20.0
DRY = -1e30
LANES = 128
ROWS = 8


def passed_along(block, axis, distance):
    devices = range(lax.axis_size(axis))
    route = [(i - distance, i) for i in devices if i - distance in devices]
    return lax.ppermute(block, axis, route)


def passed_along_2(array, axis, by):
    devices = lax.axis_size(axis)
    return lax.ppermute(array, axis, [(i, (i + by) % devices) for i in range(devices)])


def from_west(edge, column_tile):
    near = passed_along_2(edge, "space", 1)
    far = passed_along_2(edge, "space", -(TX - 1))
    return jnp.where(column_tile == 0, far, near)


def from_east(edge, column_tile):
    near = passed_along_2(edge, "space", -1)
    far = passed_along_2(edge, "space", TX - 1)
    return jnp.where(column_tile == TX - 1, far, near)


def face(depth_sum, slope):
    power = jnp.exp2(jnp.log(depth_sum) * (5.0 / 3.0 / math.log(2.0)))
    return power * slope * lax.rsqrt(jnp.abs(slope) + slope_floor)


def window_kernel(
    hours, width, rim, par_ref, d_in, s_in, g_ref, r_ref, obs_ref,
    depth_out, soak_out, miss_out, d_ref, s_ref, d_two, s_two, ge_ref, gs_ref,
):
    parts, high, wide = d_in.shape
    own_rows, own_cols = depth_out.shape[1:]
    cols = wide // LANES
    blocks = high // ROWS
    top = rim // ROWS
    bottom = top + own_rows // ROWS
    lane = lax.broadcasted_iota(jnp.int32, (ROWS, LANES), 1)
    sub = lax.broadcasted_iota(jnp.int32, (ROWS, LANES), 0)
    first_lane, last_lane = lane == 0, lane == LANES - 1
    first_sub, last_sub = sub == 0, sub == ROWS - 1

    def at(block, j):
        return pl.ds(pl.multiple_of(block * ROWS, ROWS), ROWS), pl.ds(j * LANES, LANES)

    def east(here, beside):
        return pltpu.roll(jnp.where(first_lane, beside, here), LANES - 1, 1)

    def south(here, below):
        return pltpu.roll(jnp.where(first_sub, below, here), ROWS - 1, 0)

    def prepare(block, carry):
        below = jnp.minimum(block + 1, blocks - 1)
        for j in range(cols):
            here = g_ref[at(block, j)]
            ge_ref[at(block, j)] = east(here, g_ref[at(block, (j + 1) % cols)]) - here
            gs_ref[at(block, j)] = south(here, g_ref[at(below, j)]) - here
            for p in range(parts):
                d_ref[(p,) + at(block, j)] = d_in[(p,) + at(block, j)]
                s_ref[(p,) + at(block, j)] = s_in[(p,) + at(block, j)]
        return carry

    lax.fori_loop(0, blocks, prepare, 0)
    for p in range(parts):
        d_ref[p, pl.ds(high, ROWS), :] = jnp.zeros((ROWS, wide), jnp.float32)
        d_two[p, pl.ds(high, ROWS), :] = jnp.zeros((ROWS, wide), jnp.float32)
    several = next(u for u in (4, 3, 2, 1) if blocks % u == 0)

    for hour in range(hours):

        def substep(d_old, s_old, d_new, s_new):
            def step(block, above):
                out = []
                for p in range(parts):
                    k, a, b = par_ref[0, p], par_ref[1, p], par_ref[2, p]
                    d = [d_old[(p,) + at(block, j)] for j in range(cols)]

                    def col_face(j):
                        d_e = east(d[j], d[(j + 1) % cols])
                        return face(d[j] + d_e, (d_e - d[j]) + ge_ref[at(block, j)])

                    f_col = [col_face(j) for j in range(cols)]
                    for j in range(cols):
                        f_e = f_col[j]
                        f_w = pltpu.roll(jnp.where(last_lane, f_col[j - 1], f_e), 1, 1)
                        d_s = south(d[j], d_old[(p,) + at(block + 1, j)])
                        f_s = face(d[j] + d_s, (d_s - d[j]) + gs_ref[at(block, j)])
                        f_n = pltpu.roll(jnp.where(last_sub, above[p * cols + j], f_s), 1, 0)
                        out.append(f_s)
                        gain = (f_e - f_w) + (f_s - f_n)
                        ponded = jnp.maximum(d[j] + k * gain + r_ref[(hour,) + at(block, j)], 0.0)
                        soak = s_old[(p,) + at(block, j)]
                        inverse = pl.reciprocal(soak, approx=True)
                        inverse = inverse * (2.0 - soak * inverse)
                        intake = jnp.minimum(a + b * inverse, ponded)
                        d_new[(p,) + at(block, j)] = ponded - intake
                        s_new[(p,) + at(block, j)] = soak + intake
                return tuple(out)

            def steps(index, above):
                for u in range(several):
                    above = step(index * several + u, above)
                return above

            zero = jnp.zeros((ROWS, LANES), jnp.float32)
            lax.fori_loop(0, blocks // several, steps, (zero,) * (parts * cols))

        def pair(index, carry):
            substep(d_ref, s_ref, d_two, s_two)
            substep(d_two, s_two, d_ref, s_ref)
            return carry

        lax.fori_loop(0, SUB // 2, pair, 0)

        def score(block, sums):
            sums = list(sums)
            for j in range(own_cols // LANES):
                seen = obs_ref[(hour,) + at(block, j)]
                for p in range(parts):
                    gap = d_ref[(p,) + at(block + top, j)] - seen
                    square = gap * gap
                    sums[p] += jnp.where(seen >= 0.0, square / (1.0 + square), 0.0)
            return tuple(sums)

        zero = jnp.zeros((ROWS, LANES), jnp.float32)
        sums = lax.fori_loop(0, own_rows // ROWS, score, (zero,) * parts)
        for p in range(parts):
            miss_out[p] = sums[p] if hour == 0 else miss_out[p] + sums[p]

    def finish(block, carry):
        for j in range(own_cols // LANES):
            for p in range(parts):
                depth_out[(p,) + at(block, j)] = d_ref[(p,) + at(block + top, j)]
                soak_out[(p,) + at(block, j)] = s_ref[(p,) + at(block + top, j)]
        return carry

    lax.fori_loop(0, own_rows // ROWS, finish, 0)


def weigh_kernel(n_space, n_dom, parts, mine_ref, out_ref, held, send_sem, recv_sem):
    total = n_space * n_dom
    space, dom = lax.axis_index("space"), lax.axis_index("dom")
    me = space * n_dom + dom
    barrier = pltpu.get_barrier_semaphore()

    def place(i):
        other = lax.rem(me + i, total)
        return (other // n_dom, lax.rem(other, n_dom))

    def greet(i, carry):
        pl.semaphore_signal(barrier, inc=1, device_id=place(i), device_id_type=MESH)
        return carry

    lax.fori_loop(1, total, greet, 0)
    pl.semaphore_wait(barrier, total - 1)

    def copy(i):
        return pltpu.make_async_remote_copy(
            src_ref=mine_ref, dst_ref=held.at[i], send_sem=send_sem.at[i], recv_sem=recv_sem.at[i],
            device_id=place(i), device_id_type=MESH,
        )

    def send(i, carry):
        copy(i).start()
        return carry

    def arrive(i, carry):
        copy(i).wait()
        return carry

    lax.fori_loop(1, total, send, 0)
    held[0] = mine_ref[...]
    lax.fori_loop(1, total, arrive, 0)

    def add(i, sums):
        theirs = lax.rem(lax.rem(me - i + total, total), n_dom)
        block = held[i]
        return tuple(s + jnp.where(theirs == g, block, 0.0) for g, s in enumerate(sums))

    zero = jnp.zeros(mine_ref.shape, jnp.float32)
    sums = lax.fori_loop(0, total, add, (zero,) * n_dom)
    whole = jnp.zeros((1, 1), jnp.float32)
    own = zero[0:1]
    lane = lax.broadcasted_iota(jnp.int32, (1, LANES), 1)
    for g in range(n_dom):
        misfit, cells, mean = sums[g][0:1], sums[g][1:2], sums[g][2:3] / n_space
        raw = jnp.where(lane < parts, mean * jnp.exp(-sharpness * misfit / cells), 0.0)
        whole = whole + jnp.sum(raw, axis=1, keepdims=True)
        own = jnp.where(dom == g, raw, own)
    out_ref[...] = jnp.broadcast_to(own / whole, out_ref.shape)


def local(
    n_space, n_dom,
    water_depth, infiltrated, terrain, land_mask, forcing, observed,
    conductivity, suction, manning, assignment, ancestors, prior_weight,
):
    parts, _, rows, columns = water_depth.shape
    hours = observed.shape[0]
    width = hours * SUB
    rim = -(-width // ROWS) * ROWS
    first_slot = lax.axis_index("dom") * parts
    local_slot = ancestors - first_slot
    water = jnp.take(water_depth[:, 0], local_slot, axis=0)
    soaked = jnp.take(infiltrated[:, 0], local_slot, axis=0)
    owners = jnp.take(assignment, local_slot)
    every_slot = jnp.arange(conductivity.shape[0], dtype=jnp.int32)
    picker = owners[:, None] == every_slot[None, :]

    def lookup(table):
        return jnp.sum(jnp.where(picker, table[None, :], 0.0), axis=1)

    conduct, suction_p, rough = lookup(conductivity), lookup(suction), lookup(manning)
    params = jnp.stack(
        [time_step * 0.5 ** (5.0 / 3.0) / rough, time_step * conduct, time_step * conduct * suction_p]
    )
    group_mean = jnp.mean(prior_weight)
    column_tile = lax.axis_index("space") % TX
    row_tile = lax.axis_index("space") // TX
    land = land_mask[0] > 0
    forced = lax.all_gather(forcing, "dom", axis=3, tiled=True)[:, :, 0].astype(jnp.float32)
    rain = jnp.where(land[None], time_step * (forced[:, 0] - forced[:, 1]), DRY)
    fields = jnp.concatenate([water, soaked, terrain, rain], axis=0)
    fill = jnp.array([0.0] * parts + [1.0] * parts + [0.0] + [DRY] * hours, jnp.float32)[:, None, None]
    west = from_west(fields[:, :, -width:], column_tile)
    east = from_east(fields[:, :, :width], column_tile)
    gap = jnp.broadcast_to(fill, (fields.shape[0], rows, LANES - 2 * width))
    wide = jnp.concatenate([fields, east, gap, west], axis=-1)
    north = passed_along(wide[:, -rim:, :], "space", TX)
    south = passed_along(wide[:, :rim, :], "space", -TX)
    north = jnp.where(row_tile == 0, fill, north)
    south = jnp.where(row_tile == n_space // TX - 1, fill, south)
    big = jnp.concatenate([north, wide, south], axis=-2)
    high, across = big.shape[1:]
    seen = jnp.where(land[None], observed[:, 0].astype(jnp.float32), -1.0)
    vmem = pl.BlockSpec(memory_space=pltpu.VMEM)
    depth, soak, missed = pl.pallas_call(
        functools.partial(window_kernel, hours, width, rim),
        out_shape=(
            jax.ShapeDtypeStruct((parts, rows, columns), jnp.float32),
            jax.ShapeDtypeStruct((parts, rows, columns), jnp.float32),
            jax.ShapeDtypeStruct((parts, ROWS, LANES), jnp.float32),
        ),
        in_specs=[pl.BlockSpec(memory_space=pltpu.SMEM)] + [vmem] * 5,
        out_specs=(vmem, vmem, vmem),
        scratch_shapes=[
            pltpu.VMEM((parts, high + ROWS, across), jnp.float32),
            pltpu.VMEM((parts, high, across), jnp.float32),
            pltpu.VMEM((parts, high + ROWS, across), jnp.float32),
            pltpu.VMEM((parts, high, across), jnp.float32),
            pltpu.VMEM((high, across), jnp.float32),
            pltpu.VMEM((high, across), jnp.float32),
        ],
        compiler_params=pltpu.CompilerParams(vmem_limit_bytes=48 * 2**20),
    )(params, big[:parts], big[parts : 2 * parts], big[2 * parts], big[2 * parts + 1 :], seen)
    misfit = jnp.sum(missed, axis=(1, 2))
    cells = hours * jnp.sum(land.astype(jnp.float32))
    mine = jnp.zeros((ROWS, LANES), jnp.float32).at[0, :parts].set(misfit).at[1].set(cells).at[2].set(group_mean)
    total = n_space * n_dom
    weights = pl.pallas_call(
        functools.partial(weigh_kernel, n_space, n_dom, parts),
        out_shape=jax.ShapeDtypeStruct((ROWS, LANES), jnp.float32),
        in_specs=[vmem],
        out_specs=vmem,
        scratch_shapes=[
            pltpu.VMEM((total, ROWS, LANES), jnp.float32),
            pltpu.SemaphoreType.DMA((total,)),
            pltpu.SemaphoreType.DMA((total,)),
        ],
        compiler_params=pltpu.CompilerParams(collective_id=0, has_side_effects=True),
    )(mine)
    return depth[:, None], soak[:, None], weights[0, :parts]


def solution(mesh):
    return jax.shard_map(
        functools.partial(local, mesh.shape["space"], mesh.shape["dom"]),
        mesh=mesh,
        in_specs=(
            P("dom", "space", None, None),
            P("dom", "space", None, None),
            P("space", None, None),
            P("space", None, None),
            P(None, None, "space", "dom", None),
            P(None, "space", None, None),
            P(),
            P(),
            P(),
            P("dom"),
            P("dom"),
            P("dom"),
        ),
        out_specs=(P("dom", "space", None, None), P("dom", "space", None, None), P("dom")),
        check_vma=False,
    )
```

```python
import functools
import math

import jax
import jax.numpy as jnp
from jax import lax
from jax.experimental import pallas as pl
from jax.experimental.pallas import tpu as pltpu
from jax.sharding import PartitionSpec as P

TX = 4
SUB = 6
MESH = pl.DeviceIdType.MESH

time_step = 0.01
slope_floor = 0.1
sharpness = 20.0
DRY = -1e30
LANES = 128
ROWS = 8


def passed_along(block, axis, distance):
    devices = range(lax.axis_size(axis))
    route = [(i - distance, i) for i in devices if i - distance in devices]
    return lax.ppermute(block, axis, route)


def around_row(array, axis, by):
    devices = lax.axis_size(axis)
    route = [(i, i // TX * TX + (i + by) % TX) for i in range(devices)]
    return lax.ppermute(array, axis, route)


def surrounded(fields, fill, width, rim, row_tile, last_row):
    fill = jnp.array(fill, jnp.float32)[:, None, None]
    west = around_row(fields[:, :, -width:], "space", 1)
    east = around_row(fields[:, :, :width], "space", -1)
    gap = jnp.broadcast_to(fill, (*fields.shape[:2], LANES - 2 * width))
    wide = jnp.concatenate([fields, east, gap, west], axis=-1)
    north = passed_along(wide[:, -rim:, :], "space", TX)
    south = passed_along(wide[:, :rim, :], "space", -TX)
    north = jnp.where(row_tile == 0, fill, north)
    south = jnp.where(row_tile == last_row, fill, south)
    return jnp.concatenate([north, wide, south], axis=-2)


def face(depth_sum, slope):
    power = jnp.exp2(jnp.log(depth_sum) * (5.0 / 3.0 / math.log(2.0)))
    return power * slope * lax.rsqrt(jnp.abs(slope) + slope_floor)


def window_kernel(
    hours, width, rim, par_ref, d_in, s_in, g_ref, r_ref, obs_ref,
    depth_out, soak_out, miss_out, d_ref, s_ref, d_two, s_two, ge_ref, gs_ref,
):
    parts, high, wide = d_in.shape
    own_rows, own_cols = depth_out.shape[1:]
    cols = wide // LANES
    blocks = high // ROWS
    top = rim // ROWS
    bottom = top + own_rows // ROWS
    lane = lax.broadcasted_iota(jnp.int32, (ROWS, LANES), 1)
    sub = lax.broadcasted_iota(jnp.int32, (ROWS, LANES), 0)
    first_lane, last_lane = lane == 0, lane == LANES - 1
    first_sub, last_sub = sub == 0, sub == ROWS - 1

    def at(block, j):
        return pl.ds(pl.multiple_of(block * ROWS, ROWS), ROWS), pl.ds(j * LANES, LANES)

    def east(here, beside):
        return pltpu.roll(jnp.where(first_lane, beside, here), LANES - 1, 1)

    def south(here, below):
        return pltpu.roll(jnp.where(first_sub, below, here), ROWS - 1, 0)

    def prepare(block, carry):
        below = jnp.minimum(block + 1, blocks - 1)
        for j in range(cols):
            here = g_ref[at(block, j)]
            ge_ref[at(block, j)] = east(here, g_ref[at(block, (j + 1) % cols)]) - here
            gs_ref[at(block, j)] = south(here, g_ref[at(below, j)]) - here
            for p in range(parts):
                d_ref[(p,) + at(block, j)] = d_in[(p,) + at(block, j)]
                s_ref[(p,) + at(block, j)] = s_in[(p,) + at(block, j)]
        return carry

    lax.fori_loop(0, blocks, prepare, 0)
    for p in range(parts):
        d_ref[p, pl.ds(high, ROWS), :] = jnp.zeros((ROWS, wide), jnp.float32)
        d_two[p, pl.ds(high, ROWS), :] = jnp.zeros((ROWS, wide), jnp.float32)
    several = next(u for u in (4, 3, 2, 1) if blocks % u == 0)

    for hour in range(hours):

        def substep(d_old, s_old, d_new, s_new):
            def step(block, above):
                out = []
                for p in range(parts):
                    k, a, b = par_ref[0, p], par_ref[1, p], par_ref[2, p]
                    d = [d_old[(p,) + at(block, j)] for j in range(cols)]

                    def col_face(j):
                        d_e = east(d[j], d[(j + 1) % cols])
                        return face(d[j] + d_e, (d_e - d[j]) + ge_ref[at(block, j)])

                    f_col = [col_face(j) for j in range(cols)]
                    for j in range(cols):
                        f_e = f_col[j]
                        f_w = pltpu.roll(jnp.where(last_lane, f_col[j - 1], f_e), 1, 1)
                        d_s = south(d[j], d_old[(p,) + at(block + 1, j)])
                        f_s = face(d[j] + d_s, (d_s - d[j]) + gs_ref[at(block, j)])
                        f_n = pltpu.roll(jnp.where(last_sub, above[p * cols + j], f_s), 1, 0)
                        out.append(f_s)
                        gain = (f_e - f_w) + (f_s - f_n)
                        ponded = jnp.maximum(d[j] + k * gain + r_ref[(hour,) + at(block, j)], 0.0)
                        soak = s_old[(p,) + at(block, j)]
                        inverse = pl.reciprocal(soak, approx=True)
                        inverse = inverse * (2.0 - soak * inverse)
                        intake = jnp.minimum(a + b * inverse, ponded)
                        d_new[(p,) + at(block, j)] = ponded - intake
                        s_new[(p,) + at(block, j)] = soak + intake
                return tuple(out)

            def steps(index, above):
                for u in range(several):
                    above = step(index * several + u, above)
                return above

            zero = jnp.zeros((ROWS, LANES), jnp.float32)
            lax.fori_loop(0, blocks // several, steps, (zero,) * (parts * cols))

        def pair(index, carry):
            substep(d_ref, s_ref, d_two, s_two)
            substep(d_two, s_two, d_ref, s_ref)
            return carry

        lax.fori_loop(0, SUB // 2, pair, 0)

        def score(block, sums):
            sums = list(sums)
            for j in range(own_cols // LANES):
                seen = obs_ref[(hour,) + at(block, j)]
                for p in range(parts):
                    gap = d_ref[(p,) + at(block + top, j)] - seen
                    square = gap * gap
                    sums[p] += jnp.where(seen >= 0.0, square / (1.0 + square), 0.0)
            return tuple(sums)

        zero = jnp.zeros((ROWS, LANES), jnp.float32)
        sums = lax.fori_loop(0, own_rows // ROWS, score, (zero,) * parts)
        for p in range(parts):
            miss_out[p] = sums[p] if hour == 0 else miss_out[p] + sums[p]

    def finish(block, carry):
        for j in range(own_cols // LANES):
            for p in range(parts):
                depth_out[(p,) + at(block, j)] = d_ref[(p,) + at(block + top, j)]
                soak_out[(p,) + at(block, j)] = s_ref[(p,) + at(block + top, j)]
        return carry

    lax.fori_loop(0, own_rows // ROWS, finish, 0)


def weigh_kernel(n_space, n_dom, parts, mine_ref, out_ref, held, send_sem, recv_sem):
    total = n_space * n_dom
    space, dom = lax.axis_index("space"), lax.axis_index("dom")
    me = space * n_dom + dom
    barrier = pltpu.get_barrier_semaphore()

    def place(i):
        other = lax.rem(me + i, total)
        return (other // n_dom, lax.rem(other, n_dom))

    def greet(i, carry):
        pl.semaphore_signal(barrier, inc=1, device_id=place(i), device_id_type=MESH)
        return carry

    lax.fori_loop(1, total, greet, 0)
    pl.semaphore_wait(barrier, total - 1)

    def copy(i):
        return pltpu.make_async_remote_copy(
            src_ref=mine_ref, dst_ref=held.at[i], send_sem=send_sem.at[i], recv_sem=recv_sem.at[i],
            device_id=place(i), device_id_type=MESH,
        )

    def send(i, carry):
        copy(i).start()
        return carry

    def arrive(i, carry):
        copy(i).wait()
        return carry

    lax.fori_loop(1, total, send, 0)
    held[0] = mine_ref[...]
    lax.fori_loop(1, total, arrive, 0)

    def add(i, sums):
        theirs = lax.rem(lax.rem(me - i + total, total), n_dom)
        block = held[i]
        return tuple(s + jnp.where(theirs == g, block, 0.0) for g, s in enumerate(sums))

    zero = jnp.zeros(mine_ref.shape, jnp.float32)
    sums = lax.fori_loop(0, total, add, (zero,) * n_dom)
    whole = jnp.zeros((1, 1), jnp.float32)
    own = zero[0:1]
    lane = lax.broadcasted_iota(jnp.int32, (1, LANES), 1)
    for g in range(n_dom):
        misfit, cells, mean = sums[g][0:1], sums[g][1:2], sums[g][2:3] / n_space
        raw = jnp.where(lane < parts, mean * jnp.exp(-sharpness * misfit / cells), 0.0)
        whole = whole + jnp.sum(raw, axis=1, keepdims=True)
        own = jnp.where(dom == g, raw, own)
    out_ref[...] = jnp.broadcast_to(own / whole, out_ref.shape)


def local(
    n_space, n_dom,
    water_depth, infiltrated, terrain, land_mask, forcing, observed,
    conductivity, suction, manning, assignment, ancestors, prior_weight,
):
    parts, _, rows, columns = water_depth.shape
    hours = observed.shape[0]
    width = hours * SUB
    rim = -(-width // ROWS) * ROWS
    first_slot = lax.axis_index("dom") * parts
    local_slot = ancestors - first_slot
    water = jnp.take(water_depth[:, 0], local_slot, axis=0)
    soaked = jnp.take(infiltrated[:, 0], local_slot, axis=0)
    owners = jnp.take(assignment, local_slot)
    every_slot = jnp.arange(conductivity.shape[0], dtype=jnp.int32)
    picker = owners[:, None] == every_slot[None, :]

    def lookup(table):
        return jnp.sum(jnp.where(picker, table[None, :], 0.0), axis=1)

    conduct, suction_p, rough = lookup(conductivity), lookup(suction), lookup(manning)
    params = jnp.stack(
        [time_step * 0.5 ** (5.0 / 3.0) / rough, time_step * conduct, time_step * conduct * suction_p]
    )
    group_mean = jnp.mean(prior_weight)
    row_tile = lax.axis_index("space") // TX
    land = land_mask[0] > 0
    forced = lax.all_gather(forcing, "dom", axis=3, tiled=True)[:, :, 0].astype(jnp.float32)
    rain = jnp.where(land[None], time_step * (forced[:, 0] - forced[:, 1]), DRY)
    fields = jnp.concatenate([water, soaked, terrain], axis=0)
    fill = [0.0] * parts + [1.0] * parts + [0.0]
    last_row = n_space // TX - 1
    big = surrounded(fields, fill, width, rim, row_tile, last_row)
    rain = surrounded(rain, [DRY] * hours, width, rim, row_tile, last_row)
    high, across = big.shape[1:]
    seen = jnp.where(land[None], observed[:, 0].astype(jnp.float32), -1.0)
    vmem = pl.BlockSpec(memory_space=pltpu.VMEM)
    depth, soak, missed = pl.pallas_call(
        functools.partial(window_kernel, hours, width, rim),
        out_shape=(
            jax.ShapeDtypeStruct((parts, rows, columns), jnp.float32),
            jax.ShapeDtypeStruct((parts, rows, columns), jnp.float32),
            jax.ShapeDtypeStruct((parts, ROWS, LANES), jnp.float32),
        ),
        in_specs=[pl.BlockSpec(memory_space=pltpu.SMEM)] + [vmem] * 5,
        out_specs=(vmem, vmem, vmem),
        scratch_shapes=[
            pltpu.VMEM((parts, high + ROWS, across), jnp.float32),
            pltpu.VMEM((parts, high, across), jnp.float32),
            pltpu.VMEM((parts, high + ROWS, across), jnp.float32),
            pltpu.VMEM((parts, high, across), jnp.float32),
            pltpu.VMEM((high, across), jnp.float32),
            pltpu.VMEM((high, across), jnp.float32),
        ],
        compiler_params=pltpu.CompilerParams(vmem_limit_bytes=48 * 2**20),
    )(params, big[:parts], big[parts : 2 * parts], big[2 * parts], rain, seen)
    misfit = jnp.sum(missed, axis=(1, 2))
    cells = hours * jnp.sum(land.astype(jnp.float32))
    mine = jnp.zeros((ROWS, LANES), jnp.float32).at[0, :parts].set(misfit).at[1].set(cells).at[2].set(group_mean)
    total = n_space * n_dom
    weights = pl.pallas_call(
        functools.partial(weigh_kernel, n_space, n_dom, parts),
        out_shape=jax.ShapeDtypeStruct((ROWS, LANES), jnp.float32),
        in_specs=[vmem],
        out_specs=vmem,
        scratch_shapes=[
            pltpu.VMEM((total, ROWS, LANES), jnp.float32),
            pltpu.SemaphoreType.DMA((total,)),
            pltpu.SemaphoreType.DMA((total,)),
        ],
        compiler_params=pltpu.CompilerParams(collective_id=0, has_side_effects=True),
    )(mine)
    return depth[:, None], soak[:, None], weights[0, :parts]


def solution(mesh):
    return jax.shard_map(
        functools.partial(local, mesh.shape["space"], mesh.shape["dom"]),
        mesh=mesh,
        in_specs=(
            P("dom", "space", None, None),
            P("dom", "space", None, None),
            P("space", None, None),
            P("space", None, None),
            P(None, None, "space", "dom", None),
            P(None, "space", None, None),
            P(),
            P(),
            P(),
            P("dom"),
            P("dom"),
            P("dom"),
        ),
        out_specs=(P("dom", "space", None, None), P("dom", "space", None, None), P("dom")),
        check_vma=False,
    )
```
